32 devices in a mesh: kv: 8 (over z, x), head: 4 (over y, core).
Axes of the slice: x: 2, y: 2, z: 4, core: 2. Of those that a mesh axis runs over, the one named last changes fastest.
Arguments:
- query: bfloat16 [2, 40, 128, 128], P(None, None, 'head'), may hold values from -16 to 16
- key_cache: bfloat16 [2, 8, 65536, 128], P(None, 'head', 'kv'), may hold values from -6 to 6
- value_cache: bfloat16 [2, 8, 65536, 128], P(None, 'head', 'kv'), may hold values from -6 to 6
- draft_keys: bfloat16 [2, 8, 40, 128], P(None, 'head'), may hold values from -12 to 12
- draft_values: bfloat16 [2, 8, 40, 128], P(None, 'head'), may hold values from -6 to 6
- lengths: int32 [2], replicated, may hold values from 8192 to 65536, as said below
- out_weight: bfloat16 [16384, 16384], P('head', 'kv'), may hold values from -0.1875 to 0.1875
Outputs:
- mixed: bfloat16 [2, 40, 16384], P(None, None, ('kv', 'head'))
The draws below stay inside these ranges and needn't reach their ends.
Inputs may be any that keep to these rules, and one draw needn't show every extreme that they name: `lengths`: one request has exactly 65536 cached positions.
All inputs are finite; a program needn't handle non-finite values.
Results may differ from the reference program's by a relative error of at most 0.0055.
Values may be sent and summed in bfloat16 or wider, within the bound.
A program may use at most 128 MiB of HBM per device.

```python
import math
import jax
import jax.numpy as jnp
from jax import lax

D = 16384
HEADS = 128
KV_HEADS = 8
HEAD_DIM = 128
BATCH = 2
DRAFT = 40
CONTEXT = 65536


def draw_query(key, part):
    values = jnp.clip(3.0 * jax.random.normal(jax.random.fold_in(key, 1), (BATCH, DRAFT, HEADS, HEAD_DIM), jnp.float32), -16.0, 16.0)
    return values.astype(jnp.bfloat16)


def draw_key_cache(key, part):
    values = jnp.clip(jax.random.normal(jax.random.fold_in(key, 2), (BATCH, KV_HEADS, CONTEXT, HEAD_DIM), jnp.float32), -6.0, 6.0)
    return values.astype(jnp.bfloat16)


def draw_lengths(key, part):
    base_key = jax.random.fold_in(key, 5303)
    full_key, other_key = jax.random.split(base_key, 2)
    full_request = jax.random.randint(full_key, (), 0, BATCH)
    others = jax.random.randint(other_key, (BATCH,), CONTEXT // 8, CONTEXT + 1)
    return jnp.where(jnp.arange(BATCH) == full_request, CONTEXT, others).astype(jnp.int32)


def shard_levels(rng, dims, cuts, low, high):
    level, own = 1.0, jax.random.fold_in(rng, 6)
    for position, shards_of in cuts:
        heights = jnp.exp(jax.random.uniform(jax.random.fold_in(own, position), (shards_of,), jnp.float32, low / len(cuts), high / len(cuts)))
        level = level * jnp.repeat(heights, dims[position] // shards_of).reshape([-1 if axis == position else 1 for axis in range(len(dims))])
    return level


def noise(stream_key, dims, spread, most, pieces=(), kind=jnp.bfloat16):
    loudness = shard_levels(stream_key, dims, pieces, -0.22, 0.18) if pieces else 1.0
    entries = jax.random.normal(stream_key, dims, jnp.float32) * spread * loudness
    return jnp.minimum(jnp.maximum(entries, -most), most).astype(kind)


def setup_inputs(seed: int = 0) -> dict:
    seeds = jax.random.split(jax.random.key(seed), 8)
    query = draw_query(jax.random.fold_in(seeds[7], 71), 0)
    key_cache = draw_key_cache(jax.random.fold_in(seeds[7], 71), 0)
    value_cache = noise(seeds[2], (BATCH, KV_HEADS, CONTEXT, HEAD_DIM), 1.0, 6.0, ((1, 4), (2, 8)))
    draft_keys = noise(seeds[3], (BATCH, KV_HEADS, DRAFT, HEAD_DIM), 2.0, 12.0, ((1, 4),))
    draft_values = noise(seeds[4], (BATCH, KV_HEADS, DRAFT, HEAD_DIM), 1.0, 6.0, ((1, 4),))
    lengths = draw_lengths(jax.random.fold_in(seeds[7], 71), 0)
    out_weight = noise(seeds[6], (D, D), (D // 16) ** -0.5, 0.1875, ((0, 4), (1, 8)))
    return {"query": query, "key_cache": key_cache, "value_cache": value_cache, "draft_keys": draft_keys, "draft_values": draft_values, "lengths": lengths, "out_weight": out_weight}


masked_score = -1e+30

def attend_head(queries, cached_keys, cached_values, new_keys, new_values, length):
    score_scale = 1.0 / math.sqrt(HEAD_DIM)
    query_wide = queries.astype(jnp.float32)
    cache_scores = jnp.dot(query_wide, cached_keys.astype(jnp.float32).T, preferred_element_type=jnp.float32) * score_scale
    draft_scores = jnp.dot(query_wide, new_keys.astype(jnp.float32).T, preferred_element_type=jnp.float32) * score_scale
    cache_live = (jnp.arange(CONTEXT) < length)[None, :]
    draft_live = jnp.arange(DRAFT)[None, :] <= jnp.arange(DRAFT)[:, None]
    cache_scores = jnp.where(cache_live, cache_scores, masked_score)
    draft_scores = jnp.where(draft_live, draft_scores, masked_score)
    row_max = jnp.maximum(lax.optimization_barrier(jnp.max(cache_scores, axis=1)), lax.optimization_barrier(jnp.max(draft_scores, axis=1)))
    cache_weights = jnp.where(cache_live, jnp.exp(cache_scores - row_max[:, None]), 0.0)
    draft_weights = jnp.where(draft_live, jnp.exp(draft_scores - row_max[:, None]), 0.0)
    total = lax.optimization_barrier(jnp.sum(cache_weights, axis=1)) + lax.optimization_barrier(jnp.sum(draft_weights, axis=1))
    mixture = jnp.dot(cache_weights, cached_values.astype(jnp.float32), preferred_element_type=jnp.float32)
    mixture = mixture + jnp.dot(draft_weights, new_values.astype(jnp.float32), preferred_element_type=jnp.float32)
    return mixture / total[:, None]

def reference(query, key_cache, value_cache, draft_keys, draft_values, lengths, out_weight):
    group = HEADS // KV_HEADS
    query_rows = jnp.transpose(query, (0, 2, 1, 3)).reshape(BATCH * HEADS, DRAFT, HEAD_DIM)
    flat_index = jnp.arange(BATCH * HEADS)
    owners = (flat_index // HEADS).astype(jnp.int32)
    kv_owner = (flat_index % HEADS // group).astype(jnp.int32)

    def one_head(item):
        queries, request, kv_head = item
        return attend_head(queries, key_cache[request, kv_head], value_cache[request, kv_head], draft_keys[request, kv_head], draft_values[request, kv_head], lengths[request])
    heads_out = lax.map(one_head, (query_rows, owners, kv_owner))
    attention = heads_out.reshape(BATCH, HEADS, DRAFT, HEAD_DIM)
    attention = jnp.transpose(attention, (0, 2, 1, 3)).reshape(BATCH * DRAFT, D).astype(jnp.bfloat16)
    mixed = jnp.dot(attention, out_weight, preferred_element_type=jnp.float32).astype(jnp.bfloat16)
    return mixed.reshape(BATCH, DRAFT, D)
```

```python
import functools
import math

import jax
import jax.numpy as jnp
from jax import lax
from jax.experimental import pallas as pl
from jax.experimental.pallas import tpu as pltpu
from jax.sharding import PartitionSpec as P

masked_score = -1e30
MESH = pl.DeviceIdType.MESH
f32 = jnp.float32
bf16 = jnp.bfloat16


def attend_kernel(chunk, kv_count, lengths_ref, q_ref, k_ref, v_ref, dk_ref, dv_ref, acc_out, stat_out, acc, top):
    draft, group, width = q_ref.shape[1], q_ref.shape[2], q_ref.shape[3]
    rows = draft * group
    span = k_ref.shape[2]
    request = pl.program_id(1)
    step = pl.program_id(2)
    steps = pl.num_programs(2)
    kv_index = lax.axis_index("kv")
    scale = math.log2(math.e) / math.sqrt(width)
    queries = q_ref[...].reshape(rows, width)
    chunks = rows // chunk
    contract_last = (((1,), (1,)), ((), ()))

    def scores_of(index, keys):
        part = queries[index * chunk : (index + 1) * chunk]
        return lax.dot_general(part, keys, contract_last, preferred_element_type=f32)

    def with_ones(values):
        return jnp.concatenate([values, jnp.ones(values.shape, bf16)], axis=1)

    @pl.when(step == 0)
    def _():
        keys = dk_ref[0, 0]
        values = with_ones(dv_ref[0, 0])
        for index in range(chunks):
            scores = scores_of(index, keys)
            owner = (lax.broadcasted_iota(jnp.int32, scores.shape, 0) + index * chunk) // group
            place = lax.broadcasted_iota(jnp.int32, scores.shape, 1)
            live = jnp.logical_and(place <= owner, kv_index == kv_count - 1)
            scores = jnp.where(live, scores * scale, masked_score)
            peak = jnp.max(scores, axis=1, keepdims=True)
            weights = jnp.exp2(scores - peak).astype(bf16)
            here = pl.ds(index * chunk, chunk)
            top[here, :] = jnp.broadcast_to(peak, (chunk, width))
            acc[here, :] = jnp.dot(weights, values, preferred_element_type=f32)

    first = kv_index * (span * steps) + step * span
    length = lengths_ref[request]

    def block(masked):
        keys = k_ref[0, 0]
        values = with_ones(v_ref[0, 0])
        if masked:
            live = first + lax.broadcasted_iota(jnp.int32, (1, span), 1) < length
        ahead = scores_of(0, keys)
        for index in range(chunks):
            scores = ahead
            if index + 1 < chunks:
                ahead = scores_of(index + 1, keys)
            if masked:
                scores = jnp.where(live, scores, masked_score)
            here = pl.ds(index * chunk, chunk)
            old = top[here, :]
            new = jnp.maximum(old, jnp.max(scores, axis=1, keepdims=True) * scale)
            weights = jnp.exp2(scores * scale - new[:, :1]).astype(bf16)
            factor = jnp.exp2(old - new)
            top[here, :] = new
            acc[here, :] = acc[here, :] * jnp.concatenate([factor, factor], axis=1) + jnp.dot(
                weights, values, preferred_element_type=f32
            )

    whole = first + span <= length

    @pl.when(whole)
    def _():
        block(False)

    @pl.when(jnp.logical_and(jnp.logical_not(whole), first < length))
    def _():
        block(True)

    @pl.when(step == steps - 1)
    def _():
        acc_out[0] = acc[:, :width].astype(bf16)
        share = rows // kv_count
        diagonal = lax.broadcasted_iota(jnp.int32, (share, width), 0) == lax.broadcasted_iota(
            jnp.int32, (share, width), 1
        )
        line = lax.broadcasted_iota(jnp.int32, (8, width), 0)
        for dest in range(kv_count):
            here = pl.ds(dest * share, share)
            peaks = jnp.sum(jnp.where(diagonal, top[here, :], 0.0), axis=0, keepdims=True)
            sums = jnp.sum(jnp.where(diagonal, acc[here, width:], 0.0), axis=0, keepdims=True)
            stat_out[0, dest] = jnp.where(line == 0, peaks, jnp.where(line == 1, sums, 0.0))


def attend(query, key_cache, value_cache, draft_keys, draft_values, lengths, kv_count):
    batch, draft, qheads, width = query.shape
    kv_heads, local_span = key_cache.shape[1], key_cache.shape[2]
    group = qheads // kv_heads
    rows = draft * group
    span = min(2048, local_span)
    chunk = 128 if rows % 128 == 0 else rows
    units = batch * kv_heads
    cache_spec = pl.BlockSpec((1, 1, span, width), lambda k, b, t, *_: (b, k, t, 0))
    draft_spec = pl.BlockSpec((1, 1, draft, width), lambda k, b, t, *_: (b, k, 0, 0))
    return pl.pallas_call(
        functools.partial(attend_kernel, chunk, kv_count),
        grid_spec=pltpu.PrefetchScalarGridSpec(
            num_scalar_prefetch=1,
            grid=(kv_heads, batch, local_span // span),
            in_specs=[
                pl.BlockSpec((1, draft, group, width), lambda k, b, t, *_: (b, 0, k, 0)),
                cache_spec,
                cache_spec,
                draft_spec,
                draft_spec,
            ],
            out_specs=[
                pl.BlockSpec((1, rows, width), lambda k, b, t, *_: (k * batch + b, 0, 0)),
                pl.BlockSpec((1, kv_count, 8, width), lambda k, b, t, *_: (k * batch + b, 0, 0, 0)),
            ],
            scratch_shapes=[pltpu.VMEM((rows, 2 * width), f32), pltpu.VMEM((rows, width), f32)],
        ),
        out_shape=[
            jax.ShapeDtypeStruct((units, rows, width), bf16),
            jax.ShapeDtypeStruct((units, kv_count, 8, width), f32),
        ],
        compiler_params=pltpu.CompilerParams(vmem_limit_bytes=48 * 1024 * 1024),
        cost_estimate=pl.CostEstimate(
            flops=4 * units * rows * local_span * width,
            bytes_accessed=4 * units * local_span * width,
            transcendentals=units * rows * local_span,
        ),
    )(lengths, query, key_cache, value_cache, draft_keys, draft_values)


def finish_kernel(
    kv_count, head_count, batch, group,
    acc_ref, stat_ref, w_ref, out_ref,
    weight, got_acc, got_stat, gathered, wide, lhs, sent, got_part,
    w_sem, acc_send, acc_recv, stat_send, stat_recv, near_send, far_send, gather_recv, part_send, part_recv,
):
    units, rows, width = acc_ref.shape
    share = rows // kv_count
    draft = rows // group
    columns = weight.shape[2]
    me = lax.axis_index("kv")
    head = lax.axis_index("head")

    def load(h):
        return pltpu.make_async_copy(w_ref.at[:, pl.ds(h * columns, columns)], weight.at[h], w_sem.at[h])

    for h in range(head_count):
        load(h).start()

    barrier = pltpu.get_barrier_semaphore()
    for ahead in range(1, kv_count):
        pl.semaphore_signal(barrier, inc=1, device_id={"kv": lax.rem(me + ahead, kv_count)}, device_id_type=MESH)
    for ahead in range(1, head_count):
        pl.semaphore_signal(barrier, inc=1, device_id={"head": lax.rem(head + ahead, head_count)}, device_id_type=MESH)
    pl.semaphore_wait(barrier, kv_count + head_count - 2)

    def acc_copy(dest, source):
        return pltpu.make_async_remote_copy(
            src_ref=acc_ref.at[:, pl.ds(pl.multiple_of(dest * share, 16), share), :],
            dst_ref=got_acc.at[source],
            send_sem=acc_send.at[dest],
            recv_sem=acc_recv.at[source],
            device_id={"kv": dest},
            device_id_type=MESH,
        )

    def stat_copy(dest, source):
        return pltpu.make_async_remote_copy(
            src_ref=stat_ref.at[:, dest],
            dst_ref=got_stat.at[source],
            send_sem=stat_send.at[dest],
            recv_sem=stat_recv.at[source],
            device_id={"kv": dest},
            device_id_type=MESH,
        )

    for ahead in range(1, kv_count):
        dest = lax.rem(me + ahead, kv_count)
        stat_copy(dest, me).start()
        acc_copy(dest, me).start()
    got_stat[me] = stat_ref[:, me]
    got_acc[me] = acc_ref[:, pl.ds(pl.multiple_of(me * share, 16), share), :]
    for ahead in range(1, kv_count):
        other = lax.rem(me + ahead, kv_count)
        stat_copy(other, other).wait_recv()
        acc_copy(other, other).wait_recv()

    diagonal = lax.broadcasted_iota(jnp.int32, (share, width), 0) == lax.broadcasted_iota(
        jnp.int32, (share, width), 1
    )
    for unit in range(units):
        peaks = [got_stat[source, unit][0:1, :] for source in range(kv_count)]
        peak = functools.reduce(jnp.maximum, peaks)
        factors = [jnp.exp2(value - peak) for value in peaks]
        total = sum(got_stat[source, unit][1:2, :] * factors[source] for source in range(kv_count))
        merged = jnp.zeros((share, width), f32)
        for source in range(kv_count):
            portion = jnp.broadcast_to(factors[source] / total, (share, width))
            column = jnp.sum(jnp.where(diagonal, portion, 0.0), axis=1, keepdims=True)
            merged = merged + got_acc[source, unit].astype(f32) * column
        gathered[me, unit] = merged.astype(bf16)

    partner = me + 1 - 2 * lax.rem(me, 2)
    half = kv_count // 2

    def near_copy(block):
        return pltpu.make_async_remote_copy(
            src_ref=gathered.at[block],
            dst_ref=gathered.at[block],
            send_sem=near_send.at[block],
            recv_sem=gather_recv.at[block],
            device_id={"kv": partner},
            device_id_type=MESH,
        )

    def far_copy(dest, block):
        return pltpu.make_async_remote_copy(
            src_ref=gathered.at[block],
            dst_ref=gathered.at[block],
            send_sem=far_send.at[dest],
            recv_sem=gather_recv.at[block],
            device_id={"kv": dest},
            device_id_type=MESH,
        )

    for ahead in range(1, half):
        far_copy(lax.rem(me + 2 * ahead, kv_count), me).start()
    near_copy(me).start()

    def widen(block):
        for unit in range(units):
            wide[unit, pl.ds(pl.multiple_of(block * share, 16), share), :] = gathered[block, unit].astype(f32)

    widen(me)
    for ahead in range(1, half):
        block = lax.rem(me + kv_count - 2 * ahead, kv_count)
        far_copy(block, block).wait_recv()
        near_copy(block).start()
        widen(block)
    for ahead in range(half):
        block = lax.rem(partner + kv_count - 2 * ahead, kv_count)
        near_copy(block).wait_recv()
        widen(block)

    for head_group in range(units // batch):
        for member in range(group):
            pieces = [
                wide[head_group * batch + request, pl.ds(member, draft, stride=group), :]
                for request in range(batch)
            ]
            place = (head_group * group + member) * width
            lhs[:, place : place + width] = jnp.concatenate(pieces, axis=0).astype(bf16)

    def part_copy(dest, source):
        return pltpu.make_async_remote_copy(
            src_ref=sent.at[dest],
            dst_ref=got_part.at[source],
            send_sem=part_send.at[dest],
            recv_sem=part_recv.at[source],
            device_id={"head": dest},
            device_id_type=MESH,
        )

    for h in range(head_count):
        load(h).wait()

    @pl.loop(1, head_count)
    def _(ahead):
        dest = lax.rem(head + ahead, head_count)
        sent[dest] = jnp.dot(lhs[...], weight[dest], preferred_element_type=f32).astype(bf16)
        part_copy(dest, head).start()

    result = jnp.dot(lhs[...], weight[head], preferred_element_type=f32)
    for ahead in range(1, head_count):
        source = lax.rem(head + ahead, head_count)
        part_copy(source, source).wait_recv()
        result = result + got_part[source].astype(f32)
    for request in range(batch):
        out_ref[request] = result[request * draft : (request + 1) * draft].astype(bf16)

    for ahead in range(1, kv_count):
        dest = lax.rem(me + ahead, kv_count)
        stat_copy(dest, me).wait_send()
        acc_copy(dest, me).wait_send()
    for ahead in range(1, half):
        far_copy(lax.rem(me + 2 * ahead, kv_count), me).wait_send()
    for ahead in range(half):
        near_copy(lax.rem(me + 2 * ahead, kv_count)).wait_send()
    for ahead in range(1, head_count):
        part_copy(lax.rem(head + ahead, head_count), head).wait_send()


def finish(acc, stats, out_weight, kv_count, head_count, batch, group):
    units, rows, width = acc.shape
    share = rows // kv_count
    draft = rows // group
    features, out_width = out_weight.shape
    columns = out_width // head_count
    tokens = batch * draft
    dma = pltpu.SemaphoreType.DMA
    return pl.pallas_call(
        functools.partial(finish_kernel, kv_count, head_count, batch, group),
        out_shape=jax.ShapeDtypeStruct((batch, draft, columns), bf16),
        in_specs=[
            pl.BlockSpec(memory_space=pltpu.VMEM),
            pl.BlockSpec(memory_space=pltpu.VMEM),
            pl.BlockSpec(memory_space=pl.ANY),
        ],
        out_specs=pl.BlockSpec(memory_space=pltpu.VMEM),
        scratch_shapes=[
            pltpu.VMEM((head_count, features, columns), bf16),
            pltpu.VMEM((kv_count, units, share, width), bf16),
            pltpu.VMEM((kv_count, units, 8, width), f32),
            pltpu.VMEM((kv_count, units, share, width), bf16),
            pltpu.VMEM((units, rows, width), f32),
            pltpu.VMEM((tokens, features), bf16),
            pltpu.VMEM((head_count, tokens, columns), bf16),
            pltpu.VMEM((head_count, tokens, columns), bf16),
            dma((head_count,)),
            dma((kv_count,)),
            dma((kv_count,)),
            dma((kv_count,)),
            dma((kv_count,)),
            dma((kv_count,)),
            dma((kv_count,)),
            dma((kv_count,)),
            dma((head_count,)),
            dma((head_count,)),
        ],
        compiler_params=pltpu.CompilerParams(
            collective_id=0, has_side_effects=True, vmem_limit_bytes=48 * 1024 * 1024
        ),
        cost_estimate=pl.CostEstimate(
            flops=2 * tokens * features * out_width,
            bytes_accessed=2 * features * out_width,
            transcendentals=0,
        ),
    )(acc, stats, out_weight)


def fast_per_device(query, key_cache, value_cache, draft_keys, draft_values, lengths, out_weight):
    batch, draft, qheads, width = query.shape
    group = qheads // key_cache.shape[1]
    kv_count, head_count = lax.axis_size("kv"), lax.axis_size("head")
    acc, stats = attend(query, key_cache, value_cache, draft_keys, draft_values, lengths, kv_count)
    return finish(acc, stats, out_weight, kv_count, head_count, batch, group)


def fits(query, key_cache, out_weight, kv_count, head_count):
    batch, draft, qheads, width = query.shape
    rows = draft * (qheads // key_cache.shape[1])
    share = rows // kv_count
    return (
        kv_count % 2 == 0
        and rows % kv_count == 0
        and share % 16 == 0
        and share <= width
        and width == 128
        and draft % 8 == 0
        and out_weight.shape[1] % (128 * head_count) == 0
    )


def per_device(query, key_cache, value_cache, draft_keys, draft_values, lengths, out_weight):
    if fits(query, key_cache, out_weight, lax.axis_size("kv"), lax.axis_size("head")):
        return fast_per_device(
            query, key_cache, value_cache, draft_keys, draft_values, lengths, out_weight
        )
    batch, draft, qheads, head_width = query.shape
    kv_heads = key_cache.shape[1]
    local_span = key_cache.shape[2]
    group = qheads // kv_heads
    kv_count = lax.axis_size("kv")
    kv_index = lax.axis_index("kv")
    score_scale = 1.0 / math.sqrt(head_width)
    queries = query.reshape(batch, draft, kv_heads, group, head_width)
    block_rows = min(512, local_span)
    blocks = local_span // block_rows
    start_pos = kv_index * local_span

    def absorb(state, scores, live, values):
        run_max, run_sum, mixture = state
        new_max = jnp.maximum(run_max, jnp.max(scores, axis=-1))
        weights = jnp.where(live, jnp.exp(scores - new_max[..., None]), 0.0)
        factor = jnp.exp(run_max - new_max)
        run_sum = run_sum * factor + jnp.sum(weights, axis=-1)
        mixture = mixture * factor[..., None] + jnp.einsum(
            "bkjgt,bktd->bkjgd",
            weights,
            values.astype(jnp.float32),
            preferred_element_type=jnp.float32,
        )
        return (new_max, run_sum, mixture)

    def cache_block(step_index, state):
        first_row = step_index * block_rows
        key_block = lax.dynamic_slice_in_dim(key_cache, first_row, block_rows, 2)
        value_block = lax.dynamic_slice_in_dim(value_cache, first_row, block_rows, 2)
        scores = (
            jnp.einsum("bjkgd,bktd->bkjgt", queries, key_block, preferred_element_type=jnp.float32)
            * score_scale
        )
        positions = start_pos + first_row + jnp.arange(block_rows)
        live = (positions[None, :] < lengths[:, None])[:, None, None, None, :]
        scores = jnp.where(live, scores, masked_score)
        return absorb(state, scores, live, value_block)

    stat_shape = (batch, kv_heads, draft, group)
    state = (
        jnp.full(stat_shape, masked_score, jnp.float32),
        jnp.zeros(stat_shape, jnp.float32),
        jnp.zeros(stat_shape + (head_width,), jnp.float32),
    )
    state = lax.fori_loop(0, blocks, cache_block, state)
    draft_scores = (
        jnp.einsum("bjkgd,bkid->bkjgi", queries, draft_keys, preferred_element_type=jnp.float32)
        * score_scale
    )
    causal = jnp.arange(draft)[None, :] <= jnp.arange(draft)[:, None]
    draft_live = jnp.logical_and(causal, kv_index == kv_count - 1)[None, None, :, None, :]
    draft_scores = jnp.where(draft_live, draft_scores, masked_score)
    run_max, run_sum, mixture = absorb(state, draft_scores, draft_live, draft_values)
    row_count = batch * draft
    mixture = jnp.transpose(mixture, (0, 2, 1, 3, 4)).reshape(row_count, qheads, head_width)
    run_max = jnp.transpose(run_max, (0, 2, 1, 3)).reshape(row_count, qheads)
    run_sum = jnp.transpose(run_sum, (0, 2, 1, 3)).reshape(row_count, qheads)
    feat_dev = qheads * head_width // kv_count
    unit_width = min(feat_dev, head_width)
    unit_count = head_width // unit_width
    unit_dev = feat_dev // unit_width
    sent_mix = mixture.reshape(row_count, kv_count, feat_dev)
    sent_max = jnp.repeat(run_max, unit_count, axis=1).reshape(row_count, kv_count, unit_dev)
    sent_sum = jnp.repeat(run_sum, unit_count, axis=1).reshape(row_count, kv_count, unit_dev)
    got_mix, got_max, got_sum = (
        lax.all_to_all(sent_mix, "kv", split_axis=1, concat_axis=1, tiled=True),
        lax.all_to_all(sent_max, "kv", split_axis=1, concat_axis=1, tiled=True),
        lax.all_to_all(sent_sum, "kv", split_axis=1, concat_axis=1, tiled=True),
    )
    peak = jnp.max(got_max, axis=1)
    factor = jnp.exp(got_max - peak[:, None, :])
    total = jnp.sum(got_sum * factor, axis=1)
    merged = jnp.sum(
        got_mix.reshape(row_count, kv_count, unit_dev, unit_width) * factor[..., None], axis=1
    )
    attention = (merged / total[..., None]).reshape(row_count, feat_dev).astype(jnp.bfloat16)
    partial_value = jnp.dot(
        lax.all_gather(attention, "kv", axis=1, tiled=True),
        out_weight,
        preferred_element_type=jnp.float32,
    )
    mixed = lax.psum_scatter(partial_value, "head", scatter_dimension=1, tiled=True).astype(
        jnp.bfloat16
    )
    return mixed.reshape(batch, draft, -1)


def solution(mesh):
    in_specs = (
        P(None, None, "head", None),
        P(None, "head", "kv", None),
        P(None, "head", "kv", None),
        P(None, "head", None, None),
        P(None, "head", None, None),
        P(),
        P("head", "kv"),
    )
    out_specs = P(None, None, ("kv", "head"))
    return jax.shard_map(
        per_device, mesh=mesh, in_specs=in_specs, out_specs=out_specs, check_vma=False
    )
```

```python
import functools
import math

import jax
import jax.numpy as jnp
from jax import lax
from jax.experimental import pallas as pl
from jax.experimental.pallas import tpu as pltpu
from jax.sharding import PartitionSpec as P

masked_score = -1e30
MESH = pl.DeviceIdType.MESH
f32 = jnp.float32
bf16 = jnp.bfloat16
contract_last = (((1,), (1,)), ((), ()))


def layer_kernel(
    kv_count, head_count, chunk, block, sub,
    lengths_ref, q_hbm, k_hbm, v_hbm, dk_hbm, dv_hbm, w_hbm, out_ref,
    query, keys, values, draft_keys, draft_values, weight, acc, top,
    sent_acc, sent_stat, got_acc, got_stat, gathered, wide, lhs, part, sent_part, got_part,
    small_sem, k_sem, v_sem, w_sem,
    acc_send, acc_recv, stat_send, stat_recv, gather_send, gather_recv, part_send, part_recv,
):
    batch, draft, qheads, width = query.shape
    kv_heads, local_span = k_hbm.shape[1], k_hbm.shape[2]
    group = qheads // kv_heads
    rows = draft * group
    units = batch * kv_heads
    blocks = local_span // block
    chunks = rows // chunk
    share = rows // kv_count
    columns = weight.shape[2]
    me = lax.axis_index("kv")
    head = lax.axis_index("head")
    scale = math.log2(math.e) / math.sqrt(width)

    def split(unit):
        return unit // batch, unit % batch

    def load_keys(unit, step):
        kv_head, request = split(unit)
        here = pl.ds(pl.multiple_of(step * block, block), block)
        return pltpu.make_async_copy(
            k_hbm.at[request, kv_head, here], keys.at[unit, here], k_sem.at[unit, step]
        )

    def load_values(unit, step):
        kv_head, request = split(unit)
        here = pl.ds(pl.multiple_of(step * block, block), block)
        return pltpu.make_async_copy(
            v_hbm.at[request, kv_head, here], values.at[unit, here], v_sem.at[unit, step]
        )

    def load_weight(dest):
        return pltpu.make_async_copy(
            w_hbm.at[:, pl.ds(dest * columns, columns)], weight.at[dest], w_sem.at[dest]
        )

    small = [
        pltpu.make_async_copy(source, target, small_sem.at[index])
        for index, (source, target) in enumerate(
            ((q_hbm, query), (dk_hbm, draft_keys), (dv_hbm, draft_values))
        )
    ]
    for copy in small:
        copy.start()
    for unit in range(units):
        for step in range(blocks):
            load_keys(unit, step).start()
            load_values(unit, step).start()
    for dest in range(head_count):
        load_weight(dest).start()

    barrier = pltpu.get_barrier_semaphore()
    for ahead in range(1, kv_count):
        pl.semaphore_signal(barrier, inc=1, device_id={"kv": lax.rem(me + ahead, kv_count)}, device_id_type=MESH)
    for ahead in range(1, head_count):
        pl.semaphore_signal(barrier, inc=1, device_id={"head": lax.rem(head + ahead, head_count)}, device_id_type=MESH)
    pl.semaphore_wait(barrier, kv_count + head_count - 2)
    for copy in small:
        copy.wait()

    def acc_copy(unit, dest, source):
        return pltpu.make_async_remote_copy(
            src_ref=sent_acc.at[unit, pl.ds(pl.multiple_of(dest * share, 16), share)],
            dst_ref=got_acc.at[unit, source],
            send_sem=acc_send.at[unit, dest],
            recv_sem=acc_recv.at[unit, source],
            device_id={"kv": dest},
            device_id_type=MESH,
        )

    def stat_copy(unit, dest, source):
        return pltpu.make_async_remote_copy(
            src_ref=sent_stat.at[unit, dest],
            dst_ref=got_stat.at[unit, source],
            send_sem=stat_send.at[unit, dest],
            recv_sem=stat_recv.at[unit, source],
            device_id={"kv": dest},
            device_id_type=MESH,
        )

    def gather_copy(unit, dest, source):
        return pltpu.make_async_remote_copy(
            src_ref=gathered.at[unit, source],
            dst_ref=gathered.at[unit, source],
            send_sem=gather_send.at[unit, dest],
            recv_sem=gather_recv.at[unit, source],
            device_id={"kv": dest},
            device_id_type=MESH,
        )

    def part_copy(dest, source):
        return pltpu.make_async_remote_copy(
            src_ref=sent_part.at[dest],
            dst_ref=got_part.at[source],
            send_sem=part_send.at[dest],
            recv_sem=part_recv.at[source],
            device_id={"head": dest},
            device_id_type=MESH,
        )

    def with_ones(some):
        return jnp.concatenate([some, jnp.ones(some.shape, bf16)], axis=1)

    def unit_queries(unit):
        kv_head, request = split(unit)
        some = query[request, :, pl.ds(pl.multiple_of(kv_head * group, 16), group), :]
        return some.reshape(rows, width)

    def scores_of(queries, index, some):
        mine = queries[index * chunk : (index + 1) * chunk]
        return lax.dot_general(mine, some, contract_last, preferred_element_type=f32)

    def begin(unit):
        kv_head, request = split(unit)
        queries = unit_queries(unit)
        some_keys = draft_keys[request, kv_head]
        some_values = with_ones(draft_values[request, kv_head])
        for index in range(chunks):
            scores = scores_of(queries, index, some_keys)
            owner = (lax.broadcasted_iota(jnp.int32, scores.shape, 0) + index * chunk) // group
            place = lax.broadcasted_iota(jnp.int32, scores.shape, 1)
            live = jnp.logical_and(place <= owner, me == kv_count - 1)
            scores = jnp.where(live, scores * scale, masked_score)
            peak = jnp.max(scores, axis=1, keepdims=True)
            weights = jnp.exp2(scores - peak).astype(bf16)
            here = pl.ds(index * chunk, chunk)
            top[here, :] = jnp.broadcast_to(peak, (chunk, width))
            acc[here, :] = jnp.dot(weights, some_values, preferred_element_type=f32)

    def attend(unit, step):
        queries = unit_queries(unit)
        length = lengths_ref[unit % batch]
        items = [(piece, index) for piece in range(block // sub) for index in range(chunks)]

        def scores_at(item):
            piece, index = items[item]
            start = pl.multiple_of(step * block + piece * sub, sub)
            return scores_of(queries, index, keys[unit, pl.ds(start, sub), :])

        ahead = scores_at(0)
        for item, (piece, index) in enumerate(items):
            scores = ahead
            if item + 1 < len(items):
                ahead = scores_at(item + 1)
            start = pl.multiple_of(step * block + piece * sub, sub)
            some_values = with_ones(values[unit, pl.ds(start, sub), :])
            first = me * local_span + start
            live = first + lax.broadcasted_iota(jnp.int32, (1, sub), 1) < length
            scores = jnp.where(live, scores, masked_score)
            here = pl.ds(index * chunk, chunk)
            old = top[here, :]
            new = jnp.maximum(old, jnp.max(scores, axis=1, keepdims=True) * scale)
            weights = jnp.exp2(scores * scale - new[:, :1]).astype(bf16)
            factor = jnp.exp2(old - new)
            top[here, :] = new
            acc[here, :] = acc[here, :] * jnp.concatenate([factor, factor], axis=1) + jnp.dot(
                weights, some_values, preferred_element_type=f32
            )

    diagonal = lax.broadcasted_iota(jnp.int32, (share, width), 0) == lax.broadcasted_iota(
        jnp.int32, (share, width), 1
    )
    line = lax.broadcasted_iota(jnp.int32, (8, width), 0)

    def send(unit):
        sent_acc[unit] = acc[:, :width].astype(bf16)
        for dest in range(kv_count):
            here = pl.ds(dest * share, share)
            peaks = jnp.sum(jnp.where(diagonal, top[here, :], 0.0), axis=0, keepdims=True)
            sums = jnp.sum(jnp.where(diagonal, acc[here, width:], 0.0), axis=0, keepdims=True)
            sent_stat[unit, dest] = jnp.where(line == 0, peaks, jnp.where(line == 1, sums, 0.0))
        for ahead in range(1, kv_count):
            dest = lax.rem(me + ahead, kv_count)
            stat_copy(unit, dest, me).start()
            acc_copy(unit, dest, me).start()
        got_stat[unit, me] = sent_stat[unit, me]
        got_acc[unit, me] = sent_acc[unit, pl.ds(pl.multiple_of(me * share, 16), share)]

    def merge(unit):
        for ahead in range(1, kv_count):
            other = lax.rem(me + ahead, kv_count)
            stat_copy(unit, other, other).wait_recv()
            acc_copy(unit, other, other).wait_recv()
        peaks = [got_stat[unit, source][0:1, :] for source in range(kv_count)]
        peak = functools.reduce(jnp.maximum, peaks)
        factors = [jnp.exp2(value - peak) for value in peaks]
        total = sum(got_stat[unit, source][1:2, :] * factors[source] for source in range(kv_count))
        merged = jnp.zeros((share, width), f32)
        for source in range(kv_count):
            portion = jnp.broadcast_to(factors[source] / total, (share, width))
            column = jnp.sum(jnp.where(diagonal, portion, 0.0), axis=1, keepdims=True)
            merged = merged + got_acc[unit, source].astype(f32) * column
        gathered[unit, me] = merged.astype(bf16)
        for ahead in range(1, kv_count):
            gather_copy(unit, lax.rem(me + ahead, kv_count), me).start()

    def collect(unit):
        for ahead in range(1, kv_count):
            other = lax.rem(me + ahead, kv_count)
            gather_copy(unit, other, other).wait_recv()
        for source in range(kv_count):
            wide[unit, pl.ds(source * share, share), :] = gathered[unit, source].astype(f32)

    def arrange(kv_head):
        for member in range(group):
            pieces = [
                wide[kv_head * batch + request, pl.ds(member, draft, stride=group), :]
                for request in range(batch)
            ]
            place = (kv_head * group + member) * width
            lhs[:, place : place + width] = jnp.concatenate(pieces, axis=0).astype(bf16)

    half = (kv_heads - 1) * group * width

    @pl.loop(0, units * blocks)
    def _(index):
        unit = index // blocks
        step = index % blocks

        @pl.when(step == 0)
        def _():
            begin(unit)

        @pl.when(jnp.logical_and(step == blocks - 1, unit > 0))
        def _():
            merge(unit - 1)

        load_keys(unit, step).wait()
        load_values(unit, step).wait()
        attend(unit, step)

        @pl.when(step == blocks - 1)
        def _():
            send(unit)

    for dest in range(head_count):
        load_weight(dest).wait()
    for unit in range((kv_heads - 1) * batch):
        collect(unit)
    for kv_head in range(kv_heads - 1):
        arrange(kv_head)

    @pl.loop(0, head_count)
    def _(dest):
        part[dest] = jnp.dot(lhs[:, :half], weight[dest, :half, :], preferred_element_type=f32)

    merge(units - 1)
    for unit in range((kv_heads - 1) * batch, units):
        collect(unit)
    arrange(kv_heads - 1)

    def project(dest):
        return part[dest] + jnp.dot(lhs[:, half:], weight[dest, half:, :], preferred_element_type=f32)

    @pl.loop(1, head_count)
    def _(ahead):
        dest = lax.rem(head + ahead, head_count)
        sent_part[dest] = project(dest).astype(bf16)
        part_copy(dest, head).start()

    result = project(head)
    for ahead in range(1, head_count):
        source = lax.rem(head + ahead, head_count)
        part_copy(source, source).wait_recv()
        result = result + got_part[source].astype(f32)
    for request in range(batch):
        out_ref[request] = result[request * draft : (request + 1) * draft].astype(bf16)

    @pl.loop(0, units)
    def _(unit):
        for ahead in range(1, kv_count):
            dest = lax.rem(me + ahead, kv_count)
            stat_copy(unit, dest, me).wait_send()
            acc_copy(unit, dest, me).wait_send()
            gather_copy(unit, dest, me).wait_send()

    for ahead in range(1, head_count):
        part_copy(lax.rem(head + ahead, head_count), head).wait_send()


def fast_per_device(query, key_cache, value_cache, draft_keys, draft_values, lengths, out_weight):
    batch, draft, qheads, width = query.shape
    kv_heads, local_span = key_cache.shape[1], key_cache.shape[2]
    group = qheads // kv_heads
    kv_count, head_count = lax.axis_size("kv"), lax.axis_size("head")
    rows = draft * group
    units = batch * kv_heads
    share = rows // kv_count
    features, out_width = out_weight.shape
    columns = out_width // head_count
    tokens = batch * draft
    block = min(4096, local_span)
    sub = min(2048, block)
    blocks = local_span // block
    chunk = 320 if rows % 320 == 0 else rows
    dma = pltpu.SemaphoreType.DMA
    anywhere = pl.BlockSpec(memory_space=pl.ANY)
    return pl.pallas_call(
        functools.partial(layer_kernel, kv_count, head_count, chunk, block, sub),
        out_shape=jax.ShapeDtypeStruct((batch, draft, columns), bf16),
        in_specs=[pl.BlockSpec(memory_space=pltpu.SMEM)] + [anywhere] * 6,
        out_specs=pl.BlockSpec(memory_space=pltpu.VMEM),
        scratch_shapes=[
            pltpu.VMEM(query.shape, bf16),
            pltpu.VMEM((units, local_span, width), bf16),
            pltpu.VMEM((units, local_span, width), bf16),
            pltpu.VMEM(draft_keys.shape, bf16),
            pltpu.VMEM(draft_values.shape, bf16),
            pltpu.VMEM((head_count, features, columns), bf16),
            pltpu.VMEM((rows, 2 * width), f32),
            pltpu.VMEM((rows, width), f32),
            pltpu.VMEM((units, rows, width), bf16),
            pltpu.VMEM((units, kv_count, 8, width), f32),
            pltpu.VMEM((units, kv_count, share, width), bf16),
            pltpu.VMEM((units, kv_count, 8, width), f32),
            pltpu.VMEM((units, kv_count, share, width), bf16),
            pltpu.VMEM((units, rows, width), f32),
            pltpu.VMEM((tokens, features), bf16),
            pltpu.VMEM((head_count, tokens, columns), f32),
            pltpu.VMEM((head_count, tokens, columns), bf16),
            pltpu.VMEM((head_count, tokens, columns), bf16),
            dma((3,)),
            dma((units, blocks)),
            dma((units, blocks)),
            dma((head_count,)),
        ]
        + [dma((units, kv_count))] * 6
        + [dma((head_count,))] * 2,
        compiler_params=pltpu.CompilerParams(
            collective_id=0, has_side_effects=True, vmem_limit_bytes=60 * 1024 * 1024
        ),
        cost_estimate=pl.CostEstimate(
            flops=4 * units * rows * local_span * width + 2 * tokens * features * out_width,
            bytes_accessed=4 * units * local_span * width + 2 * features * out_width,
            transcendentals=units * rows * local_span,
        ),
    )(lengths, query, key_cache, value_cache, draft_keys, draft_values, out_weight)


def fits(query, key_cache, out_weight, kv_count, head_count):
    batch, draft, qheads, width = query.shape
    kv_heads, local_span = key_cache.shape[1], key_cache.shape[2]
    group = qheads // kv_heads
    rows = draft * group
    share = rows // kv_count
    held = 4 * batch * kv_heads * local_span * width + 2 * math.prod(out_weight.shape)
    return (
        rows % kv_count == 0
        and share % 16 == 0
        and share <= width
        and width == 128
        and draft % 8 == 0
        and group % 16 == 0
        and kv_heads > 1
        and local_span % 4096 == 0
        and held <= 36 * 1024 * 1024
        and out_weight.shape[1] % (128 * head_count) == 0
    )


def per_device(query, key_cache, value_cache, draft_keys, draft_values, lengths, out_weight):
    if fits(query, key_cache, out_weight, lax.axis_size("kv"), lax.axis_size("head")):
        return fast_per_device(
            query, key_cache, value_cache, draft_keys, draft_values, lengths, out_weight
        )
    batch, draft, qheads, head_width = query.shape
    kv_heads = key_cache.shape[1]
    local_span = key_cache.shape[2]
    group = qheads // kv_heads
    kv_count = lax.axis_size("kv")
    kv_index = lax.axis_index("kv")
    score_scale = 1.0 / math.sqrt(head_width)
    queries = query.reshape(batch, draft, kv_heads, group, head_width)
    block_rows = min(512, local_span)
    blocks = local_span // block_rows
    start_pos = kv_index * local_span

    def absorb(state, scores, live, values):
        run_max, run_sum, mixture = state
        new_max = jnp.maximum(run_max, jnp.max(scores, axis=-1))
        weights = jnp.where(live, jnp.exp(scores - new_max[..., None]), 0.0)
        factor = jnp.exp(run_max - new_max)
        run_sum = run_sum * factor + jnp.sum(weights, axis=-1)
        mixture = mixture * factor[..., None] + jnp.einsum(
            "bkjgt,bktd->bkjgd",
            weights,
            values.astype(jnp.float32),
            preferred_element_type=jnp.float32,
        )
        return (new_max, run_sum, mixture)

    def cache_block(step_index, state):
        first_row = step_index * block_rows
        key_block = lax.dynamic_slice_in_dim(key_cache, first_row, block_rows, 2)
        value_block = lax.dynamic_slice_in_dim(value_cache, first_row, block_rows, 2)
        scores = (
            jnp.einsum("bjkgd,bktd->bkjgt", queries, key_block, preferred_element_type=jnp.float32)
            * score_scale
        )
        positions = start_pos + first_row + jnp.arange(block_rows)
        live = (positions[None, :] < lengths[:, None])[:, None, None, None, :]
        scores = jnp.where(live, scores, masked_score)
        return absorb(state, scores, live, value_block)

    stat_shape = (batch, kv_heads, draft, group)
    state = (
        jnp.full(stat_shape, masked_score, jnp.float32),
        jnp.zeros(stat_shape, jnp.float32),
        jnp.zeros(stat_shape + (head_width,), jnp.float32),
    )
    state = lax.fori_loop(0, blocks, cache_block, state)
    draft_scores = (
        jnp.einsum("bjkgd,bkid->bkjgi", queries, draft_keys, preferred_element_type=jnp.float32)
        * score_scale
    )
    causal = jnp.arange(draft)[None, :] <= jnp.arange(draft)[:, None]
    draft_live = jnp.logical_and(causal, kv_index == kv_count - 1)[None, None, :, None, :]
    draft_scores = jnp.where(draft_live, draft_scores, masked_score)
    run_max, run_sum, mixture = absorb(state, draft_scores, draft_live, draft_values)
    row_count = batch * draft
    mixture = jnp.transpose(mixture, (0, 2, 1, 3, 4)).reshape(row_count, qheads, head_width)
    run_max = jnp.transpose(run_max, (0, 2, 1, 3)).reshape(row_count, qheads)
    run_sum = jnp.transpose(run_sum, (0, 2, 1, 3)).reshape(row_count, qheads)
    feat_dev = qheads * head_width // kv_count
    unit_width = min(feat_dev, head_width)
    unit_count = head_width // unit_width
    unit_dev = feat_dev // unit_width
    sent_mix = mixture.reshape(row_count, kv_count, feat_dev)
    sent_max = jnp.repeat(run_max, unit_count, axis=1).reshape(row_count, kv_count, unit_dev)
    sent_sum = jnp.repeat(run_sum, unit_count, axis=1).reshape(row_count, kv_count, unit_dev)
    got_mix, got_max, got_sum = (
        lax.all_to_all(sent_mix, "kv", split_axis=1, concat_axis=1, tiled=True),
        lax.all_to_all(sent_max, "kv", split_axis=1, concat_axis=1, tiled=True),
        lax.all_to_all(sent_sum, "kv", split_axis=1, concat_axis=1, tiled=True),
    )
    peak = jnp.max(got_max, axis=1)
    factor = jnp.exp(got_max - peak[:, None, :])
    total = jnp.sum(got_sum * factor, axis=1)
    merged = jnp.sum(
        got_mix.reshape(row_count, kv_count, unit_dev, unit_width) * factor[..., None], axis=1
    )
    attention = (merged / total[..., None]).reshape(row_count, feat_dev).astype(jnp.bfloat16)
    partial_value = jnp.dot(
        lax.all_gather(attention, "kv", axis=1, tiled=True),
        out_weight,
        preferred_element_type=jnp.float32,
    )
    mixed = lax.psum_scatter(partial_value, "head", scatter_dimension=1, tiled=True).astype(
        jnp.bfloat16
    )
    return mixed.reshape(batch, draft, -1)


def solution(mesh):
    in_specs = (
        P(None, None, "head", None),
        P(None, "head", "kv", None),
        P(None, "head", "kv", None),
        P(None, "head", None, None),
        P(None, "head", None, None),
        P(),
        P("head", "kv"),
    )
    out_specs = P(None, None, ("kv", "head"))
    return jax.shard_map(
        per_device, mesh=mesh, in_specs=in_specs, out_specs=out_specs, check_vma=False
    )
```

```python
import functools
import math

import jax
import jax.numpy as jnp
from jax import lax
from jax.experimental import pallas as pl
from jax.experimental.pallas import tpu as pltpu
from jax.sharding import PartitionSpec as P

masked_score = -1e30
MESH = pl.DeviceIdType.MESH
f32 = jnp.float32
bf16 = jnp.bfloat16
contract_last = (((1,), (1,)), ((), ()))


def layer_kernel(
    kv_count, head_count, chunk, block, sub, tile_width,
    lengths_ref, q_hbm, k_hbm, v_hbm, dk_hbm, dv_hbm, w_hbm, out_ref,
    query, keys, values, draft_keys, draft_values, weight, acc, top, next_scores, next_highest,
    sent_acc, sent_stat, got_acc, got_stat, gathered, wide, lhs, part, sent_part, got_part,
    small_sem, k_sem, v_sem, w_sem,
    acc_send, acc_recv, stat_send, stat_recv, gather_send, gather_recv, part_send, part_recv,
):
    batch, draft, qheads, width = query.shape
    kv_heads, local_span = k_hbm.shape[1], k_hbm.shape[2]
    group = qheads // kv_heads
    rows = draft * group
    units = batch * kv_heads
    blocks = local_span // block
    chunks = rows // chunk
    share = rows // kv_count
    columns = weight.shape[2]
    me = lax.axis_index("kv")
    head = lax.axis_index("head")
    scale = math.log2(math.e) / math.sqrt(width)

    def split(unit):
        return unit // batch, unit % batch

    def load_keys(unit, step):
        kv_head, request = split(unit)
        here = pl.ds(pl.multiple_of(step * block, block), block)
        return pltpu.make_async_copy(
            k_hbm.at[request, kv_head, here], keys.at[unit, here], k_sem.at[unit, step]
        )

    def load_values(unit, step):
        kv_head, request = split(unit)
        here = pl.ds(pl.multiple_of(step * block, block), block)
        return pltpu.make_async_copy(
            v_hbm.at[request, kv_head, here], values.at[unit, here], v_sem.at[unit, step]
        )

    def load_weight(dest):
        return pltpu.make_async_copy(
            w_hbm.at[:, pl.ds(dest * columns, columns)], weight.at[dest], w_sem.at[dest]
        )

    small = [
        pltpu.make_async_copy(source, target, small_sem.at[index])
        for index, (source, target) in enumerate(
            ((q_hbm, query), (dk_hbm, draft_keys), (dv_hbm, draft_values))
        )
    ]
    for copy in small:
        copy.start()
    for unit in range(units):
        for step in range(blocks):
            load_keys(unit, step).start()
            load_values(unit, step).start()
    for dest in range(head_count):
        load_weight(dest).start()

    barrier = pltpu.get_barrier_semaphore()
    for ahead in range(1, kv_count):
        pl.semaphore_signal(barrier, inc=1, device_id={"kv": lax.rem(me + ahead, kv_count)}, device_id_type=MESH)
    for ahead in range(1, head_count):
        pl.semaphore_signal(barrier, inc=1, device_id={"head": lax.rem(head + ahead, head_count)}, device_id_type=MESH)
    pl.semaphore_wait(barrier, kv_count + head_count - 2)
    for copy in small:
        copy.wait()

    def acc_copy(unit, dest, source):
        return pltpu.make_async_remote_copy(
            src_ref=sent_acc.at[unit, pl.ds(pl.multiple_of(dest * share, 16), share)],
            dst_ref=got_acc.at[unit, source],
            send_sem=acc_send.at[unit, dest],
            recv_sem=acc_recv.at[unit, source],
            device_id={"kv": dest},
            device_id_type=MESH,
        )

    def stat_copy(unit, dest, source):
        return pltpu.make_async_remote_copy(
            src_ref=sent_stat.at[unit, dest],
            dst_ref=got_stat.at[unit, source],
            send_sem=stat_send.at[unit, dest],
            recv_sem=stat_recv.at[unit, source],
            device_id={"kv": dest},
            device_id_type=MESH,
        )

    def gather_copy(unit, dest, source):
        return pltpu.make_async_remote_copy(
            src_ref=gathered.at[unit, source],
            dst_ref=gathered.at[unit, source],
            send_sem=gather_send.at[unit, dest],
            recv_sem=gather_recv.at[unit, source],
            device_id={"kv": dest},
            device_id_type=MESH,
        )

    def part_copy(dest, source):
        return pltpu.make_async_remote_copy(
            src_ref=sent_part.at[dest],
            dst_ref=got_part.at[source],
            send_sem=part_send.at[dest],
            recv_sem=part_recv.at[source],
            device_id={"head": dest},
            device_id_type=MESH,
        )

    def with_ones(some):
        return jnp.concatenate([some, jnp.ones(some.shape, bf16)], axis=1)

    def unit_queries(unit):
        kv_head, request = split(unit)
        some = query[request, :, pl.ds(pl.multiple_of(kv_head * group, 16), group), :]
        return some.reshape(rows, width)

    def scores_of(queries, index, some):
        mine = queries[index * chunk : (index + 1) * chunk]
        return lax.dot_general(mine, some, contract_last, preferred_element_type=f32)

    def begin(unit):
        kv_head, request = split(unit)
        queries = unit_queries(unit)
        some_keys = draft_keys[request, kv_head]
        some_values = with_ones(draft_values[request, kv_head])
        for index in range(chunks):
            scores = scores_of(queries, index, some_keys)
            owner = (lax.broadcasted_iota(jnp.int32, scores.shape, 0) + index * chunk) // group
            place = lax.broadcasted_iota(jnp.int32, scores.shape, 1)
            live = jnp.logical_and(place <= owner, me == kv_count - 1)
            scores = jnp.where(live, scores * scale, masked_score)
            peak = jnp.max(scores, axis=1, keepdims=True)
            weights = jnp.exp2(scores - peak).astype(bf16)
            here = pl.ds(index * chunk, chunk)
            top[here, :] = jnp.broadcast_to(peak, (chunk, width))
            acc[here, :] = jnp.dot(weights, some_values, preferred_element_type=f32)

    def score_tile(unit, step, piece, index, tile):
        start = pl.multiple_of(step * block + piece * sub + tile * tile_width, tile_width)
        scores = scores_of(unit_queries(unit), index, keys[unit, pl.ds(start, tile_width), :])
        first = me * local_span + start
        live = first + lax.broadcasted_iota(jnp.int32, (1, tile_width), 1) < lengths_ref[unit % batch]
        return jnp.where(live, scores, masked_score)

    def lane_max(known, scores):
        for lane in range(0, tile_width, width):
            here = scores[:, lane : lane + width]
            known = here if known is None else jnp.maximum(known, here)
        return known

    tiles = sub // tile_width

    def prime():
        highest = None
        for tile in range(tiles):
            scores = score_tile(0, 0, 0, 0, tile)
            highest = lane_max(highest, scores)
            next_scores[:, tile * tile_width : (tile + 1) * tile_width] = scores
        next_highest[...] = highest

    def attend(unit, step, next_unit, next_step):
        items = [(piece, index) for piece in range(block // sub) for index in range(chunks)]
        current = [next_scores[:, tile * tile_width : (tile + 1) * tile_width] for tile in range(tiles)]
        highest = next_highest[...]
        for item, (piece, index) in enumerate(items):
            last = item + 1 == len(items)
            if last:
                following = (next_unit, next_step, 0, 0)
            else:
                following = (unit, step) + items[item + 1]
            here = pl.ds(index * chunk, chunk)
            old = top[here, :]
            new = jnp.maximum(old, jnp.max(highest, axis=1, keepdims=True) * scale)
            factor = jnp.exp2(old - new)
            top[here, :] = new
            edge = new[:, :1]
            mixture = acc[here, :] * jnp.concatenate([factor, factor], axis=1)
            produced, highest = [], None
            for tile in range(tiles):
                scores = score_tile(*following, tile)
                highest = lane_max(highest, scores)
                weights = jnp.exp2(current[tile] * scale - edge).astype(bf16)
                start = pl.multiple_of(step * block + piece * sub + tile * tile_width, tile_width)
                mixture = mixture + jnp.dot(
                    weights,
                    with_ones(values[unit, pl.ds(start, tile_width), :]),
                    preferred_element_type=f32,
                )
                produced.append(scores)
            acc[here, :] = mixture
            current = produced
        for tile in range(tiles):
            next_scores[:, tile * tile_width : (tile + 1) * tile_width] = current[tile]
        next_highest[...] = highest

    diagonal = lax.broadcasted_iota(jnp.int32, (share, width), 0) == lax.broadcasted_iota(
        jnp.int32, (share, width), 1
    )
    line = lax.broadcasted_iota(jnp.int32, (8, width), 0)

    def send(unit):
        sent_acc[unit] = acc[:, :width].astype(bf16)
        for dest in range(kv_count):
            here = pl.ds(dest * share, share)
            peaks = jnp.sum(jnp.where(diagonal, top[here, :], 0.0), axis=0, keepdims=True)
            sums = jnp.sum(jnp.where(diagonal, acc[here, width:], 0.0), axis=0, keepdims=True)
            sent_stat[unit, dest] = jnp.where(line == 0, peaks, jnp.where(line == 1, sums, 0.0))
        for ahead in range(1, kv_count):
            dest = lax.rem(me + ahead, kv_count)
            stat_copy(unit, dest, me).start()
            acc_copy(unit, dest, me).start()
        got_stat[unit, me] = sent_stat[unit, me]
        got_acc[unit, me] = sent_acc[unit, pl.ds(pl.multiple_of(me * share, 16), share)]

    def merge(unit):
        for ahead in range(1, kv_count):
            other = lax.rem(me + ahead, kv_count)
            stat_copy(unit, other, other).wait_recv()
            acc_copy(unit, other, other).wait_recv()
        peaks = [got_stat[unit, source][0:1, :] for source in range(kv_count)]
        peak = functools.reduce(jnp.maximum, peaks)
        factors = [jnp.exp2(value - peak) for value in peaks]
        total = sum(got_stat[unit, source][1:2, :] * factors[source] for source in range(kv_count))
        merged = jnp.zeros((share, width), f32)
        for source in range(kv_count):
            portion = jnp.broadcast_to(factors[source] / total, (share, width))
            column = jnp.sum(jnp.where(diagonal, portion, 0.0), axis=1, keepdims=True)
            merged = merged + got_acc[unit, source].astype(f32) * column
        gathered[unit, me] = merged.astype(bf16)
        for ahead in range(1, kv_count):
            gather_copy(unit, lax.rem(me + ahead, kv_count), me).start()

    def collect(unit):
        for ahead in range(1, kv_count):
            other = lax.rem(me + ahead, kv_count)
            gather_copy(unit, other, other).wait_recv()
        for source in range(kv_count):
            wide[unit, pl.ds(source * share, share), :] = gathered[unit, source].astype(f32)

    def arrange(kv_head):
        for member in range(group):
            pieces = [
                wide[kv_head * batch + request, pl.ds(member, draft, stride=group), :]
                for request in range(batch)
            ]
            place = (kv_head * group + member) * width
            lhs[:, place : place + width] = jnp.concatenate(pieces, axis=0).astype(bf16)

    half = (kv_heads - 1) * group * width

    load_keys(0, 0).wait()
    prime()

    @pl.loop(0, units * blocks)
    def _(index):
        unit = index // blocks
        step = index % blocks

        @pl.when(step == 0)
        def _():
            begin(unit)

        @pl.when(jnp.logical_and(step == blocks - 1, unit > 0))
        def _():
            merge(unit - 1)

        following = lax.rem(index + 1, units * blocks)

        @pl.when(following > 0)
        def _():
            load_keys(following // blocks, following % blocks).wait()

        load_values(unit, step).wait()
        attend(unit, step, following // blocks, following % blocks)

        @pl.when(step == blocks - 1)
        def _():
            send(unit)

    for dest in range(head_count):
        load_weight(dest).wait()
    for unit in range((kv_heads - 1) * batch):
        collect(unit)
    for kv_head in range(kv_heads - 1):
        arrange(kv_head)

    @pl.loop(0, head_count)
    def _(dest):
        part[dest] = jnp.dot(lhs[:, :half], weight[dest, :half, :], preferred_element_type=f32)

    merge(units - 1)
    for unit in range((kv_heads - 1) * batch, units):
        collect(unit)
    arrange(kv_heads - 1)

    def project(dest):
        return part[dest] + jnp.dot(lhs[:, half:], weight[dest, half:, :], preferred_element_type=f32)

    @pl.loop(1, head_count)
    def _(ahead):
        dest = lax.rem(head + ahead, head_count)
        sent_part[dest] = project(dest).astype(bf16)
        part_copy(dest, head).start()

    result = project(head)
    for ahead in range(1, head_count):
        source = lax.rem(head + ahead, head_count)
        part_copy(source, source).wait_recv()
        result = result + got_part[source].astype(f32)
    for request in range(batch):
        out_ref[request] = result[request * draft : (request + 1) * draft].astype(bf16)

    @pl.loop(0, units)
    def _(unit):
        for ahead in range(1, kv_count):
            dest = lax.rem(me + ahead, kv_count)
            stat_copy(unit, dest, me).wait_send()
            acc_copy(unit, dest, me).wait_send()
            gather_copy(unit, dest, me).wait_send()

    for ahead in range(1, head_count):
        part_copy(lax.rem(head + ahead, head_count), head).wait_send()


def fast_per_device(query, key_cache, value_cache, draft_keys, draft_values, lengths, out_weight):
    batch, draft, qheads, width = query.shape
    kv_heads, local_span = key_cache.shape[1], key_cache.shape[2]
    group = qheads // kv_heads
    kv_count, head_count = lax.axis_size("kv"), lax.axis_size("head")
    rows = draft * group
    units = batch * kv_heads
    share = rows // kv_count
    features, out_width = out_weight.shape
    columns = out_width // head_count
    tokens = batch * draft
    block = min(4096, local_span)
    sub = min(2048, block)
    tile_width = min(1024, sub)
    blocks = local_span // block
    chunk = 320 if rows % 320 == 0 else rows
    dma = pltpu.SemaphoreType.DMA
    anywhere = pl.BlockSpec(memory_space=pl.ANY)
    return pl.pallas_call(
        functools.partial(layer_kernel, kv_count, head_count, chunk, block, sub, tile_width),
        out_shape=jax.ShapeDtypeStruct((batch, draft, columns), bf16),
        in_specs=[pl.BlockSpec(memory_space=pltpu.SMEM)] + [anywhere] * 6,
        out_specs=pl.BlockSpec(memory_space=pltpu.VMEM),
        scratch_shapes=[
            pltpu.VMEM(query.shape, bf16),
            pltpu.VMEM((units, local_span, width), bf16),
            pltpu.VMEM((units, local_span, width), bf16),
            pltpu.VMEM(draft_keys.shape, bf16),
            pltpu.VMEM(draft_values.shape, bf16),
            pltpu.VMEM((head_count, features, columns), bf16),
            pltpu.VMEM((rows, 2 * width), f32),
            pltpu.VMEM((rows, width), f32),
            pltpu.VMEM((chunk, sub), f32),
            pltpu.VMEM((chunk, width), f32),
            pltpu.VMEM((units, rows, width), bf16),
            pltpu.VMEM((units, kv_count, 8, width), f32),
            pltpu.VMEM((units, kv_count, share, width), bf16),
            pltpu.VMEM((units, kv_count, 8, width), f32),
            pltpu.VMEM((units, kv_count, share, width), bf16),
            pltpu.VMEM((units, rows, width), f32),
            pltpu.VMEM((tokens, features), bf16),
            pltpu.VMEM((head_count, tokens, columns), f32),
            pltpu.VMEM((head_count, tokens, columns), bf16),
            pltpu.VMEM((head_count, tokens, columns), bf16),
            dma((3,)),
            dma((units, blocks)),
            dma((units, blocks)),
            dma((head_count,)),
        ]
        + [dma((units, kv_count))] * 6
        + [dma((head_count,))] * 2,
        compiler_params=pltpu.CompilerParams(
            collective_id=0, has_side_effects=True, vmem_limit_bytes=60 * 1024 * 1024
        ),
        cost_estimate=pl.CostEstimate(
            flops=4 * units * rows * local_span * width + 2 * tokens * features * out_width,
            bytes_accessed=4 * units * local_span * width + 2 * features * out_width,
            transcendentals=units * rows * local_span,
        ),
    )(lengths, query, key_cache, value_cache, draft_keys, draft_values, out_weight)


def fits(query, key_cache, out_weight, kv_count, head_count):
    batch, draft, qheads, width = query.shape
    kv_heads, local_span = key_cache.shape[1], key_cache.shape[2]
    group = qheads // kv_heads
    rows = draft * group
    share = rows // kv_count
    held = 4 * batch * kv_heads * local_span * width + 2 * math.prod(out_weight.shape)
    return (
        rows % kv_count == 0
        and share % 16 == 0
        and share <= width
        and width == 128
        and draft % 8 == 0
        and group % 16 == 0
        and kv_heads > 1
        and local_span % 4096 == 0
        and held <= 36 * 1024 * 1024
        and out_weight.shape[1] % (128 * head_count) == 0
    )


def per_device(query, key_cache, value_cache, draft_keys, draft_values, lengths, out_weight):
    if fits(query, key_cache, out_weight, lax.axis_size("kv"), lax.axis_size("head")):
        return fast_per_device(
            query, key_cache, value_cache, draft_keys, draft_values, lengths, out_weight
        )
    batch, draft, qheads, head_width = query.shape
    kv_heads = key_cache.shape[1]
    local_span = key_cache.shape[2]
    group = qheads // kv_heads
    kv_count = lax.axis_size("kv")
    kv_index = lax.axis_index("kv")
    score_scale = 1.0 / math.sqrt(head_width)
    queries = query.reshape(batch, draft, kv_heads, group, head_width)
    block_rows = min(512, local_span)
    blocks = local_span // block_rows
    start_pos = kv_index * local_span

    def absorb(state, scores, live, values):
        run_max, run_sum, mixture = state
        new_max = jnp.maximum(run_max, jnp.max(scores, axis=-1))
        weights = jnp.where(live, jnp.exp(scores - new_max[..., None]), 0.0)
        factor = jnp.exp(run_max - new_max)
        run_sum = run_sum * factor + jnp.sum(weights, axis=-1)
        mixture = mixture * factor[..., None] + jnp.einsum(
            "bkjgt,bktd->bkjgd",
            weights,
            values.astype(jnp.float32),
            preferred_element_type=jnp.float32,
        )
        return (new_max, run_sum, mixture)

    def cache_block(step_index, state):
        first_row = step_index * block_rows
        key_block = lax.dynamic_slice_in_dim(key_cache, first_row, block_rows, 2)
        value_block = lax.dynamic_slice_in_dim(value_cache, first_row, block_rows, 2)
        scores = (
            jnp.einsum("bjkgd,bktd->bkjgt", queries, key_block, preferred_element_type=jnp.float32)
            * score_scale
        )
        positions = start_pos + first_row + jnp.arange(block_rows)
        live = (positions[None, :] < lengths[:, None])[:, None, None, None, :]
        scores = jnp.where(live, scores, masked_score)
        return absorb(state, scores, live, value_block)

    stat_shape = (batch, kv_heads, draft, group)
    state = (
        jnp.full(stat_shape, masked_score, jnp.float32),
        jnp.zeros(stat_shape, jnp.float32),
        jnp.zeros(stat_shape + (head_width,), jnp.float32),
    )
    state = lax.fori_loop(0, blocks, cache_block, state)
    draft_scores = (
        jnp.einsum("bjkgd,bkid->bkjgi", queries, draft_keys, preferred_element_type=jnp.float32)
        * score_scale
    )
    causal = jnp.arange(draft)[None, :] <= jnp.arange(draft)[:, None]
    draft_live = jnp.logical_and(causal, kv_index == kv_count - 1)[None, None, :, None, :]
    draft_scores = jnp.where(draft_live, draft_scores, masked_score)
    run_max, run_sum, mixture = absorb(state, draft_scores, draft_live, draft_values)
    row_count = batch * draft
    mixture = jnp.transpose(mixture, (0, 2, 1, 3, 4)).reshape(row_count, qheads, head_width)
    run_max = jnp.transpose(run_max, (0, 2, 1, 3)).reshape(row_count, qheads)
    run_sum = jnp.transpose(run_sum, (0, 2, 1, 3)).reshape(row_count, qheads)
    feat_dev = qheads * head_width // kv_count
    unit_width = min(feat_dev, head_width)
    unit_count = head_width // unit_width
    unit_dev = feat_dev // unit_width
    sent_mix = mixture.reshape(row_count, kv_count, feat_dev)
    sent_max = jnp.repeat(run_max, unit_count, axis=1).reshape(row_count, kv_count, unit_dev)
    sent_sum = jnp.repeat(run_sum, unit_count, axis=1).reshape(row_count, kv_count, unit_dev)
    got_mix, got_max, got_sum = (
        lax.all_to_all(sent_mix, "kv", split_axis=1, concat_axis=1, tiled=True),
        lax.all_to_all(sent_max, "kv", split_axis=1, concat_axis=1, tiled=True),
        lax.all_to_all(sent_sum, "kv", split_axis=1, concat_axis=1, tiled=True),
    )
    peak = jnp.max(got_max, axis=1)
    factor = jnp.exp(got_max - peak[:, None, :])
    total = jnp.sum(got_sum * factor, axis=1)
    merged = jnp.sum(
        got_mix.reshape(row_count, kv_count, unit_dev, unit_width) * factor[..., None], axis=1
    )
    attention = (merged / total[..., None]).reshape(row_count, feat_dev).astype(jnp.bfloat16)
    partial_value = jnp.dot(
        lax.all_gather(attention, "kv", axis=1, tiled=True),
        out_weight,
        preferred_element_type=jnp.float32,
    )
    mixed = lax.psum_scatter(partial_value, "head", scatter_dimension=1, tiled=True).astype(
        jnp.bfloat16
    )
    return mixed.reshape(batch, draft, -1)


def solution(mesh):
    in_specs = (
        P(None, None, "head", None),
        P(None, "head", "kv", None),
        P(None, "head", "kv", None),
        P(None, "head", None, None),
        P(None, "head", None, None),
        P(),
        P("head", "kv"),
    )
    out_specs = P(None, None, ("kv", "head"))
    return jax.shard_map(
        per_device, mesh=mesh, in_specs=in_specs, out_specs=out_specs, check_vma=False
    )
```

```python
import functools
import math

import jax
import jax.numpy as jnp
from jax import lax
from jax.experimental import pallas as pl
from jax.experimental.pallas import tpu as pltpu
from jax.sharding import PartitionSpec as P

masked_score = -1e30
MESH = pl.DeviceIdType.MESH
f32 = jnp.float32
bf16 = jnp.bfloat16
contract_last = (((1,), (1,)), ((), ()))


def layer_kernel(
    kv_count, head_count, chunk, block, sub,
    lengths_ref, q_hbm, k_hbm, v_hbm, dk_hbm, dv_hbm, w_hbm, out_ref,
    query, keys, values, draft_keys, draft_values, weight, acc, top,
    sent_acc, sent_stat, got_acc, got_stat, gathered, wide, lhs, part, sent_part, got_part,
    small_sem, k_sem, v_sem, w_sem,
    acc_send, acc_recv, stat_send, stat_recv, gather_send, gather_recv, part_send, part_recv,
):
    batch, draft, qheads, width = query.shape
    kv_heads, local_span = k_hbm.shape[1], k_hbm.shape[2]
    group = qheads // kv_heads
    rows = draft * group
    units = batch * kv_heads
    blocks = local_span // block
    chunks = rows // chunk
    share = rows // kv_count
    columns = weight.shape[2]
    me = lax.axis_index("kv")
    head = lax.axis_index("head")
    scale = math.log2(math.e) / math.sqrt(width)

    def split(unit):
        return unit // batch, unit % batch

    def load_keys(unit, step):
        kv_head, request = split(unit)
        here = pl.ds(pl.multiple_of(step * block, block), block)
        return pltpu.make_async_copy(
            k_hbm.at[request, kv_head, here], keys.at[unit, here], k_sem.at[unit, step]
        )

    def load_values(unit, step):
        kv_head, request = split(unit)
        here = pl.ds(pl.multiple_of(step * block, block), block)
        return pltpu.make_async_copy(
            v_hbm.at[request, kv_head, here], values.at[unit, here], v_sem.at[unit, step]
        )

    def load_weight(dest):
        return pltpu.make_async_copy(
            w_hbm.at[:, pl.ds(dest * columns, columns)], weight.at[dest], w_sem.at[dest]
        )

    small = [
        pltpu.make_async_copy(source, target, small_sem.at[index])
        for index, (source, target) in enumerate(
            ((q_hbm, query), (dk_hbm, draft_keys), (dv_hbm, draft_values))
        )
    ]
    for copy in small:
        copy.start()
    for unit in range(units):
        for step in range(blocks):
            load_keys(unit, step).start()
            load_values(unit, step).start()
    for dest in range(head_count):
        load_weight(dest).start()

    barrier = pltpu.get_barrier_semaphore()
    for ahead in range(1, kv_count):
        pl.semaphore_signal(barrier, inc=1, device_id={"kv": lax.rem(me + ahead, kv_count)}, device_id_type=MESH)
    for ahead in range(1, head_count):
        pl.semaphore_signal(barrier, inc=1, device_id={"head": lax.rem(head + ahead, head_count)}, device_id_type=MESH)
    pl.semaphore_wait(barrier, kv_count + head_count - 2)
    for copy in small:
        copy.wait()

    def acc_copy(unit, dest, source):
        return pltpu.make_async_remote_copy(
            src_ref=sent_acc.at[unit, pl.ds(pl.multiple_of(dest * share, 16), share)],
            dst_ref=got_acc.at[unit, source],
            send_sem=acc_send.at[unit, dest],
            recv_sem=acc_recv.at[unit, source],
            device_id={"kv": dest},
            device_id_type=MESH,
        )

    def stat_copy(unit, dest, source):
        return pltpu.make_async_remote_copy(
            src_ref=sent_stat.at[unit, dest],
            dst_ref=got_stat.at[unit, source],
            send_sem=stat_send.at[unit, dest],
            recv_sem=stat_recv.at[unit, source],
            device_id={"kv": dest},
            device_id_type=MESH,
        )

    def gather_copy(unit, dest, source):
        return pltpu.make_async_remote_copy(
            src_ref=gathered.at[unit, source],
            dst_ref=gathered.at[unit, source],
            send_sem=gather_send.at[unit, dest],
            recv_sem=gather_recv.at[unit, source],
            device_id={"kv": dest},
            device_id_type=MESH,
        )

    def part_copy(dest, source):
        return pltpu.make_async_remote_copy(
            src_ref=sent_part.at[dest],
            dst_ref=got_part.at[source],
            send_sem=part_send.at[dest],
            recv_sem=part_recv.at[source],
            device_id={"head": dest},
            device_id_type=MESH,
        )

    def with_ones(some):
        return jnp.concatenate([some, jnp.ones(some.shape, bf16)], axis=1)

    def unit_queries(unit):
        kv_head, request = split(unit)
        some = query[request, :, pl.ds(pl.multiple_of(kv_head * group, 16), group), :]
        return some.reshape(rows, width)

    def scores_of(queries, index, some):
        mine = queries[index * chunk : (index + 1) * chunk]
        return lax.dot_general(mine, some, contract_last, preferred_element_type=f32)

    def begin(unit):
        kv_head, request = split(unit)
        queries = unit_queries(unit)
        some_keys = draft_keys[request, kv_head]
        some_values = with_ones(draft_values[request, kv_head])
        for index in range(chunks):
            scores = scores_of(queries, index, some_keys)
            owner = (lax.broadcasted_iota(jnp.int32, scores.shape, 0) + index * chunk) // group
            place = lax.broadcasted_iota(jnp.int32, scores.shape, 1)
            live = jnp.logical_and(place <= owner, me == kv_count - 1)
            scores = jnp.where(live, scores * scale, masked_score)
            peak = jnp.max(scores, axis=1, keepdims=True)
            weights = jnp.exp2(scores - peak).astype(bf16)
            here = pl.ds(index * chunk, chunk)
            top[here, :] = jnp.broadcast_to(peak, (chunk, width))
            acc[here, :] = jnp.dot(weights, some_values, preferred_element_type=f32)

    def attend(unit, step):
        queries = unit_queries(unit)
        length = lengths_ref[unit % batch]
        items = [(piece, index) for piece in range(block // sub) for index in range(chunks)]

        def scores_at(item):
            piece, index = items[item]
            start = pl.multiple_of(step * block + piece * sub, sub)
            return scores_of(queries, index, keys[unit, pl.ds(start, sub), :])

        ahead = scores_at(0)
        for item, (piece, index) in enumerate(items):
            scores = ahead
            if item + 1 < len(items):
                ahead = scores_at(item + 1)
            start = pl.multiple_of(step * block + piece * sub, sub)
            some_values = with_ones(values[unit, pl.ds(start, sub), :])
            first = me * local_span + start
            live = first + lax.broadcasted_iota(jnp.int32, (1, sub), 1) < length
            scores = scores + jnp.where(live, 0.0, masked_score)
            here = pl.ds(index * chunk, chunk)
            old = top[here, :]
            new = jnp.maximum(old, jnp.max(scores, axis=1, keepdims=True) * scale)
            weights = jnp.exp2(scores * scale - new[:, :1]).astype(bf16)
            factor = jnp.exp2(old - new)
            top[here, :] = new
            acc[here, :] = acc[here, :] * jnp.concatenate([factor, factor], axis=1) + jnp.dot(
                weights, some_values, preferred_element_type=f32
            )

    diagonal = lax.broadcasted_iota(jnp.int32, (share, width), 0) == lax.broadcasted_iota(
        jnp.int32, (share, width), 1
    )
    line = lax.broadcasted_iota(jnp.int32, (8, width), 0)

    def send(unit):
        sent_acc[unit] = acc[:, :width].astype(bf16)
        for dest in range(kv_count):
            here = pl.ds(dest * share, share)
            peaks = jnp.sum(jnp.where(diagonal, top[here, :], 0.0), axis=0, keepdims=True)
            sums = jnp.sum(jnp.where(diagonal, acc[here, width:], 0.0), axis=0, keepdims=True)
            sent_stat[unit, dest] = jnp.where(line == 0, peaks, jnp.where(line == 1, sums, 0.0))
        for ahead in range(1, kv_count):
            dest = lax.rem(me + ahead, kv_count)
            stat_copy(unit, dest, me).start()
            acc_copy(unit, dest, me).start()
        got_stat[unit, me] = sent_stat[unit, me]
        got_acc[unit, me] = sent_acc[unit, pl.ds(pl.multiple_of(me * share, 16), share)]

    def merge(unit):
        for ahead in range(1, kv_count):
            other = lax.rem(me + ahead, kv_count)
            stat_copy(unit, other, other).wait_recv()
            acc_copy(unit, other, other).wait_recv()
        peaks = [got_stat[unit, source][0:1, :] for source in range(kv_count)]
        peak = functools.reduce(jnp.maximum, peaks)
        factors = [jnp.exp2(value - peak) for value in peaks]
        total = sum(got_stat[unit, source][1:2, :] * factors[source] for source in range(kv_count))
        merged = jnp.zeros((share, width), f32)
        for source in range(kv_count):
            portion = jnp.broadcast_to(factors[source] / total, (share, width))
            column = jnp.sum(jnp.where(diagonal, portion, 0.0), axis=1, keepdims=True)
            merged = merged + got_acc[unit, source].astype(f32) * column
        gathered[unit, me] = merged.astype(bf16)
        for ahead in range(1, kv_count):
            gather_copy(unit, lax.rem(me + ahead, kv_count), me).start()

    def collect(unit):
        for ahead in range(1, kv_count):
            other = lax.rem(me + ahead, kv_count)
            gather_copy(unit, other, other).wait_recv()
        for source in range(kv_count):
            wide[unit, pl.ds(source * share, share), :] = gathered[unit, source].astype(f32)

    def arrange(kv_head):
        for member in range(group):
            pieces = [
                wide[kv_head * batch + request, pl.ds(member, draft, stride=group), :]
                for request in range(batch)
            ]
            place = (kv_head * group + member) * width
            lhs[:, place : place + width] = jnp.concatenate(pieces, axis=0).astype(bf16)

    half = (kv_heads - 1) * group * width

    @pl.loop(0, units * blocks)
    def _(index):
        unit = index // blocks
        step = index % blocks

        @pl.when(step == 0)
        def _():
            begin(unit)

        @pl.when(jnp.logical_and(step == blocks - 1, unit > 0))
        def _():
            merge(unit - 1)

        load_keys(unit, step).wait()
        load_values(unit, step).wait()
        attend(unit, step)

        @pl.when(step == blocks - 1)
        def _():
            send(unit)

    for dest in range(head_count):
        load_weight(dest).wait()
    for unit in range((kv_heads - 1) * batch):
        collect(unit)
    for kv_head in range(kv_heads - 1):
        arrange(kv_head)

    @pl.loop(0, head_count)
    def _(dest):
        part[dest] = jnp.dot(lhs[:, :half], weight[dest, :half, :], preferred_element_type=f32)

    merge(units - 1)
    for unit in range((kv_heads - 1) * batch, units):
        collect(unit)
    arrange(kv_heads - 1)

    def project(dest):
        return part[dest] + jnp.dot(lhs[:, half:], weight[dest, half:, :], preferred_element_type=f32)

    @pl.loop(1, head_count)
    def _(ahead):
        dest = lax.rem(head + ahead, head_count)
        sent_part[dest] = project(dest).astype(bf16)
        part_copy(dest, head).start()

    result = project(head)
    for ahead in range(1, head_count):
        source = lax.rem(head + ahead, head_count)
        part_copy(source, source).wait_recv()
        result = result + got_part[source].astype(f32)
    for request in range(batch):
        out_ref[request] = result[request * draft : (request + 1) * draft].astype(bf16)

    @pl.loop(0, units)
    def _(unit):
        for ahead in range(1, kv_count):
            dest = lax.rem(me + ahead, kv_count)
            stat_copy(unit, dest, me).wait_send()
            acc_copy(unit, dest, me).wait_send()
            gather_copy(unit, dest, me).wait_send()

    for ahead in range(1, head_count):
        part_copy(lax.rem(head + ahead, head_count), head).wait_send()


def fast_per_device(query, key_cache, value_cache, draft_keys, draft_values, lengths, out_weight):
    batch, draft, qheads, width = query.shape
    kv_heads, local_span = key_cache.shape[1], key_cache.shape[2]
    group = qheads // kv_heads
    kv_count, head_count = lax.axis_size("kv"), lax.axis_size("head")
    rows = draft * group
    units = batch * kv_heads
    share = rows // kv_count
    features, out_width = out_weight.shape
    columns = out_width // head_count
    tokens = batch * draft
    block = min(4096, local_span)
    sub = min(2048, block)
    blocks = local_span // block
    chunk = 320 if rows % 320 == 0 else rows
    dma = pltpu.SemaphoreType.DMA
    anywhere = pl.BlockSpec(memory_space=pl.ANY)
    return pl.pallas_call(
        functools.partial(layer_kernel, kv_count, head_count, chunk, block, sub),
        out_shape=jax.ShapeDtypeStruct((batch, draft, columns), bf16),
        in_specs=[pl.BlockSpec(memory_space=pltpu.SMEM)] + [anywhere] * 6,
        out_specs=pl.BlockSpec(memory_space=pltpu.VMEM),
        scratch_shapes=[
            pltpu.VMEM(query.shape, bf16),
            pltpu.VMEM((units, local_span, width), bf16),
            pltpu.VMEM((units, local_span, width), bf16),
            pltpu.VMEM(draft_keys.shape, bf16),
            pltpu.VMEM(draft_values.shape, bf16),
            pltpu.VMEM((head_count, features, columns), bf16),
            pltpu.VMEM((rows, 2 * width), f32),
            pltpu.VMEM((rows, width), f32),
            pltpu.VMEM((units, rows, width), bf16),
            pltpu.VMEM((units, kv_count, 8, width), f32),
            pltpu.VMEM((units, kv_count, share, width), bf16),
            pltpu.VMEM((units, kv_count, 8, width), f32),
            pltpu.VMEM((units, kv_count, share, width), bf16),
            pltpu.VMEM((units, rows, width), f32),
            pltpu.VMEM((tokens, features), bf16),
            pltpu.VMEM((head_count, tokens, columns), f32),
            pltpu.VMEM((head_count, tokens, columns), bf16),
            pltpu.VMEM((head_count, tokens, columns), bf16),
            dma((3,)),
            dma((units, blocks)),
            dma((units, blocks)),
            dma((head_count,)),
        ]
        + [dma((units, kv_count))] * 6
        + [dma((head_count,))] * 2,
        compiler_params=pltpu.CompilerParams(
            collective_id=0, has_side_effects=True, vmem_limit_bytes=60 * 1024 * 1024
        ),
        cost_estimate=pl.CostEstimate(
            flops=4 * units * rows * local_span * width + 2 * tokens * features * out_width,
            bytes_accessed=4 * units * local_span * width + 2 * features * out_width,
            transcendentals=units * rows * local_span,
        ),
    )(lengths, query, key_cache, value_cache, draft_keys, draft_values, out_weight)


def fits(query, key_cache, out_weight, kv_count, head_count):
    batch, draft, qheads, width = query.shape
    kv_heads, local_span = key_cache.shape[1], key_cache.shape[2]
    group = qheads // kv_heads
    rows = draft * group
    share = rows // kv_count
    held = 4 * batch * kv_heads * local_span * width + 2 * math.prod(out_weight.shape)
    return (
        rows % kv_count == 0
        and share % 16 == 0
        and share <= width
        and width == 128
        and draft % 8 == 0
        and group % 16 == 0
        and kv_heads > 1
        and local_span % 4096 == 0
        and held <= 36 * 1024 * 1024
        and out_weight.shape[1] % (128 * head_count) == 0
    )


def per_device(query, key_cache, value_cache, draft_keys, draft_values, lengths, out_weight):
    if fits(query, key_cache, out_weight, lax.axis_size("kv"), lax.axis_size("head")):
        return fast_per_device(
            query, key_cache, value_cache, draft_keys, draft_values, lengths, out_weight
        )
    batch, draft, qheads, head_width = query.shape
    kv_heads = key_cache.shape[1]
    local_span = key_cache.shape[2]
    group = qheads // kv_heads
    kv_count = lax.axis_size("kv")
    kv_index = lax.axis_index("kv")
    score_scale = 1.0 / math.sqrt(head_width)
    queries = query.reshape(batch, draft, kv_heads, group, head_width)
    block_rows = min(512, local_span)
    blocks = local_span // block_rows
    start_pos = kv_index * local_span

    def absorb(state, scores, live, values):
        run_max, run_sum, mixture = state
        new_max = jnp.maximum(run_max, jnp.max(scores, axis=-1))
        weights = jnp.where(live, jnp.exp(scores - new_max[..., None]), 0.0)
        factor = jnp.exp(run_max - new_max)
        run_sum = run_sum * factor + jnp.sum(weights, axis=-1)
        mixture = mixture * factor[..., None] + jnp.einsum(
            "bkjgt,bktd->bkjgd",
            weights,
            values.astype(jnp.float32),
            preferred_element_type=jnp.float32,
        )
        return (new_max, run_sum, mixture)

    def cache_block(step_index, state):
        first_row = step_index * block_rows
        key_block = lax.dynamic_slice_in_dim(key_cache, first_row, block_rows, 2)
        value_block = lax.dynamic_slice_in_dim(value_cache, first_row, block_rows, 2)
        scores = (
            jnp.einsum("bjkgd,bktd->bkjgt", queries, key_block, preferred_element_type=jnp.float32)
            * score_scale
        )
        positions = start_pos + first_row + jnp.arange(block_rows)
        live = (positions[None, :] < lengths[:, None])[:, None, None, None, :]
        scores = jnp.where(live, scores, masked_score)
        return absorb(state, scores, live, value_block)

    stat_shape = (batch, kv_heads, draft, group)
    state = (
        jnp.full(stat_shape, masked_score, jnp.float32),
        jnp.zeros(stat_shape, jnp.float32),
        jnp.zeros(stat_shape + (head_width,), jnp.float32),
    )
    state = lax.fori_loop(0, blocks, cache_block, state)
    draft_scores = (
        jnp.einsum("bjkgd,bkid->bkjgi", queries, draft_keys, preferred_element_type=jnp.float32)
        * score_scale
    )
    causal = jnp.arange(draft)[None, :] <= jnp.arange(draft)[:, None]
    draft_live = jnp.logical_and(causal, kv_index == kv_count - 1)[None, None, :, None, :]
    draft_scores = jnp.where(draft_live, draft_scores, masked_score)
    run_max, run_sum, mixture = absorb(state, draft_scores, draft_live, draft_values)
    row_count = batch * draft
    mixture = jnp.transpose(mixture, (0, 2, 1, 3, 4)).reshape(row_count, qheads, head_width)
    run_max = jnp.transpose(run_max, (0, 2, 1, 3)).reshape(row_count, qheads)
    run_sum = jnp.transpose(run_sum, (0, 2, 1, 3)).reshape(row_count, qheads)
    feat_dev = qheads * head_width // kv_count
    unit_width = min(feat_dev, head_width)
    unit_count = head_width // unit_width
    unit_dev = feat_dev // unit_width
    sent_mix = mixture.reshape(row_count, kv_count, feat_dev)
    sent_max = jnp.repeat(run_max, unit_count, axis=1).reshape(row_count, kv_count, unit_dev)
    sent_sum = jnp.repeat(run_sum, unit_count, axis=1).reshape(row_count, kv_count, unit_dev)
    got_mix, got_max, got_sum = (
        lax.all_to_all(sent_mix, "kv", split_axis=1, concat_axis=1, tiled=True),
        lax.all_to_all(sent_max, "kv", split_axis=1, concat_axis=1, tiled=True),
        lax.all_to_all(sent_sum, "kv", split_axis=1, concat_axis=1, tiled=True),
    )
    peak = jnp.max(got_max, axis=1)
    factor = jnp.exp(got_max - peak[:, None, :])
    total = jnp.sum(got_sum * factor, axis=1)
    merged = jnp.sum(
        got_mix.reshape(row_count, kv_count, unit_dev, unit_width) * factor[..., None], axis=1
    )
    attention = (merged / total[..., None]).reshape(row_count, feat_dev).astype(jnp.bfloat16)
    partial_value = jnp.dot(
        lax.all_gather(attention, "kv", axis=1, tiled=True),
        out_weight,
        preferred_element_type=jnp.float32,
    )
    mixed = lax.psum_scatter(partial_value, "head", scatter_dimension=1, tiled=True).astype(
        jnp.bfloat16
    )
    return mixed.reshape(batch, draft, -1)


def solution(mesh):
    in_specs = (
        P(None, None, "head", None),
        P(None, "head", "kv", None),
        P(None, "head", "kv", None),
        P(None, "head", None, None),
        P(None, "head", None, None),
        P(),
        P("head", "kv"),
    )
    out_specs = P(None, None, ("kv", "head"))
    return jax.shard_map(
        per_device, mesh=mesh, in_specs=in_specs, out_specs=out_specs, check_vma=False
    )
```
